128 devices in a mesh: sub: 2 (over z_hi), vox: 64 (over y, x, z_lo, core).
Axes of the slice: x: 4, y: 4, z: 4 (z_hi: 2, z_lo: 2; z = z_hi * 2 + z_lo), core: 2. Of those that a mesh axis runs over, the one named last changes fastest.
Arguments:
- observed: float32 [2048, 131072], P('sub', 'vox'), may hold values from -6 to 6
- covariates: float32 [2048, 64], P('sub'), may hold values from -0.26516504 to 0.26516504
- voxel_mask: int32 [131072], P('vox'), may hold values 0 or 1
- tau_index: int32 [1], replicated, may hold values from 2 to 18
Outputs:
- coefficients: float32 [64, 131072], P(None, 'vox')
- split_residual: float32 [2048, 131072], P('sub', 'vox')
The draws below stay inside these ranges and needn't reach their ends.
All inputs are finite; a program needn't handle non-finite values. Where the reference program divides by a largest or mean magnitude, that divisor is 1e-20 or more. No bound on the sum of `voxel_mask` on one device may be relied on, other than what follows from the above.
Results may differ from the reference program's by a relative error of at most 0.0001.
Values sent between devices are 32-bit elements; how exact they have to be, the bound alone decides.
A program may use at most 128 MiB of HBM per device.

```python
import jax
import jax.numpy as jnp
from jax import lax

COVARS = 64
PX = 8
PY = 8
GZ = 32
NPY = 8
ITERS = 3
QUANT = 20
NPX = 8
GX = 64
GY = 64
VOXELS = 131072
SUBJECTS = 2048


def draw_covariates(key, part):
    scale_key = jax.random.fold_in(key, 11)
    value_key = jax.random.fold_in(key, 12)
    scales = jnp.exp(jax.random.uniform(scale_key, (COVARS,), jnp.float32, jnp.log(0.3), jnp.log(3.0)))
    values = jnp.clip(jax.random.normal(value_key, (SUBJECTS, COVARS), jnp.float32), -4.0, 4.0)
    return values * scales[None, :] / jnp.sqrt(jnp.float32(SUBJECTS))


def plant(array, rng, least, largest):
    shape = array.shape
    index_at = [jax.random.randint(jax.random.fold_in(rng, axis), (), 0, shape[axis]) for axis in range(len(shape))]
    array = array.at[tuple(index_at)].set(least)
    longest = shape.index(max(shape))
    index_at[longest] = (index_at[longest] + 1) % shape[longest]
    return array.at[tuple(index_at)].set(largest)


def shard_levels(own_key, shape, split, low, largest):
    def one(position, shards_of):
        draws = jax.random.uniform(jax.random.fold_in(jax.random.fold_in(own_key, 6), position), (shards_of,), jnp.float32, low / len(split), largest / len(split))
        return jnp.repeat(jnp.exp(draws), shape[position] // shards_of).reshape((-1,) + (1,) * (len(shape) - position - 1))

    level = one(*split[0])
    for cut in split[1:]:
        level = level * one(*cut)
    return level


def gaussian(own_key, shape, scale, most, cuts=(), held_as=jnp.bfloat16):
    gain = shard_levels(own_key, shape, cuts, -0.22, 0.18) if cuts else 1.0
    drawn = jax.random.normal(own_key, shape, jnp.float32) * scale * gain
    return jnp.minimum(jnp.maximum(drawn, -most), most).astype(held_as)


def setup_inputs(seed: int = 0) -> dict:
    splits = jax.random.split(jax.random.key(seed), 5)
    return {
        "observed": gaussian(splits[0], (SUBJECTS, VOXELS), 1.0, 6.0, ((0, 2), (1, 64)), jnp.float32),
        "covariates": draw_covariates(jax.random.fold_in(splits[4], 71), 0),
        "voxel_mask": plant((jax.random.randint(splits[2], (VOXELS,), 0, 4) < 3).astype(jnp.int32), jax.random.fold_in(splits[2], 1), 0, 1),
        "tau_index": jax.random.randint(splits[3], (1,), 2, 19).astype(jnp.int32),
    }


penalty_fit = 1.0
penalty_tv = 1.0
tv_weight = 0.05
huber_width = 0.02


def to_grid(flat):
    leading = flat.shape[:-1]
    lead_rank = len(leading)
    blocks = flat.reshape(leading + (NPX * NPY, PX * PY * GZ))
    blocks = jnp.roll(blocks, NPY // 2, axis=lead_rank)
    axis_order = tuple(range(lead_rank)) + (lead_rank, lead_rank + 2, lead_rank + 1, lead_rank + 3, lead_rank + 4)
    pieces = blocks.reshape(leading + (NPX, NPY, PX, PY, GZ)).transpose(axis_order)
    return pieces.reshape(leading + (GX, GY, GZ))


def to_flat(volume):
    leading = volume.shape[:-3]
    lead_rank = len(leading)
    axis_order = tuple(range(lead_rank)) + (lead_rank, lead_rank + 2, lead_rank + 1, lead_rank + 3, lead_rank + 4)
    pieces = volume.reshape(leading + (NPX, PX, NPY, PY, GZ)).transpose(axis_order)
    blocks = pieces.reshape(leading + (NPX * NPY, PX * PY * GZ))
    blocks = jnp.roll(blocks, -(NPY // 2), axis=lead_rank)
    return blocks.reshape(leading + (VOXELS,))


def shift_next(field, along):
    extent = field.shape[along]
    later = lax.slice_in_dim(field, 1, extent, axis=along)
    padding = jnp.zeros_like(lax.slice_in_dim(field, 0, 1, axis=along))
    return jnp.concatenate([later, padding], along)


def shift_prev(field, along):
    extent = field.shape[along]
    earlier = lax.slice_in_dim(field, 0, extent - 1, axis=along)
    padding = jnp.zeros_like(lax.slice_in_dim(field, 0, 1, axis=along))
    return jnp.concatenate([padding, earlier], along)


def forward(volume):
    results = [jnp.roll(volume, -1, axis=1) - volume]
    for along in (2, 3):
        places = lax.broadcasted_iota(jnp.int32, volume.shape, along)
        inner = (places < volume.shape[along] - 1).astype(volume.dtype)
        results.append(inner * (shift_next(volume, along) - volume))
    return jnp.stack(results)


def adjoint(dual_tv):
    summed = jnp.roll(dual_tv[0], 1, axis=1) - dual_tv[0]
    summed = summed + (shift_prev(dual_tv[1], 2) - dual_tv[1])
    summed = summed + (shift_prev(dual_tv[2], 3) - dual_tv[2])
    return summed


def huber_prox(target):
    clip_bound = tv_weight / penalty_tv
    return target - jnp.clip(target * (clip_bound / (huber_width + clip_bound)), -clip_bound, clip_bound)


def first_sums(observed, covariates, masked):
    highest = lax.Precision.HIGHEST
    block = PX * PY * GZ

    def one_block(index, summed):
        start = (index * block).astype(jnp.int32)
        rows = lax.dynamic_slice_in_dim(observed, start, block, 1)
        mask_block = lax.dynamic_slice_in_dim(masked, start, block, 0)[None, :]
        term = jnp.dot(covariates.T, mask_block * rows, precision=highest)
        return lax.dynamic_update_slice_in_dim(summed, term, start, 1)

    initial = jnp.zeros((COVARS, VOXELS), jnp.float32)
    return lax.fori_loop(0, VOXELS // block, one_block, initial)


def state_pass(observed, covariates, masked, flat_coeffs, split_res, scaled_dual, summed, quantile, want_next):
    highest = lax.Precision.HIGHEST
    block = PX * PY * GZ

    def one_block(index, carry):
        split_res, scaled_dual, summed = carry
        start = (index * block).astype(jnp.int32)
        rows = lax.dynamic_slice_in_dim(observed, start, block, 1)
        mask_block = lax.dynamic_slice_in_dim(masked, start, block, 0)[None, :]
        coef_block = lax.dynamic_slice_in_dim(flat_coeffs, start, block, 1)
        fitted = rows - jnp.dot(covariates, coef_block, precision=highest)
        old_dual = lax.dynamic_slice_in_dim(scaled_dual, start, block, 1)
        target = fitted + old_dual
        new_split = mask_block * (target - jnp.clip(target, (quantile - 1.0) / penalty_fit, quantile / penalty_fit))
        new_dual = old_dual + mask_block * (fitted - new_split)
        split_res = lax.dynamic_update_slice_in_dim(split_res, new_split, start, 1)
        scaled_dual = lax.dynamic_update_slice_in_dim(scaled_dual, new_dual, start, 1)
        if want_next:
            misfit = mask_block * (fitted - new_split + new_dual)
            term = jnp.dot(covariates.T, misfit, precision=highest)
            summed = lax.dynamic_update_slice_in_dim(summed, term, start, 1)
        return split_res, scaled_dual, summed

    return lax.fori_loop(0, VOXELS // block, one_block, (split_res, scaled_dual, summed))


def reference(observed, covariates, voxel_mask, tau_index):
    highest = lax.Precision.HIGHEST
    quantile = tau_index[0].astype(jnp.float32) / QUANT
    gram_matrix = jnp.dot(covariates.T, covariates, precision=highest)
    row_bound = jnp.max(jnp.sum(jnp.abs(gram_matrix), axis=1))
    step_size = 1.0 / (penalty_fit * row_bound + 12.0 * penalty_tv)
    masked = voxel_mask.astype(jnp.float32)
    coeffs = jnp.zeros((COVARS, GX, GY, GZ), jnp.float32)
    differences = jnp.zeros((3, COVARS, GX, GY, GZ), jnp.float32)
    split_tv = jnp.zeros((3, COVARS, GX, GY, GZ), jnp.float32)
    tv_dual = jnp.zeros((3, COVARS, GX, GY, GZ), jnp.float32)
    split_res = jnp.zeros_like(observed)
    scaled_dual = jnp.zeros_like(observed)
    summed_flat = first_sums(observed, covariates, masked)
    for iteration in range(ITERS):
        dual_tv = differences - split_tv + tv_dual
        coeffs = coeffs - step_size * (-penalty_fit * to_grid(summed_flat) + penalty_tv * adjoint(dual_tv))
        flat_coeffs = to_flat(coeffs)
        split_res, scaled_dual, summed_flat = state_pass(observed, covariates, masked, flat_coeffs, split_res, scaled_dual, summed_flat, quantile, iteration + 1 < ITERS)
        differences = forward(coeffs)
        target_tv = differences + tv_dual
        split_tv = huber_prox(target_tv)
        tv_dual = tv_dual + differences - split_tv
    return to_flat(coeffs), split_res
```

```python
import functools

import jax
import jax.numpy as jnp
from jax import lax
from jax.experimental import pallas as pl
from jax.experimental.pallas import tpu as pltpu
from jax.sharding import PartitionSpec as P

COVARS = 64
PX = 8
PY = 8
GZ = 32
NPY = 8
QUANT = 20
LAYER = PY * GZ
ROWS = 256

penalty_fit = 1.0
penalty_tv = 1.0
tv_weight = 0.05
huber_width = 0.02
BOUND = tv_weight / penalty_tv
RATIO = BOUND / (huber_width + BOUND)

MESH = pl.DeviceIdType.MESH
F32 = jnp.float32
BF16 = jnp.bfloat16


def halves(value):
    high = value.astype(BF16)
    return high, (value - high.astype(F32)).astype(BF16)


def product(left, right):
    return jnp.dot(left, right, preferred_element_type=F32)


def stacked(coef):
    high, low = halves(coef)
    return jnp.concatenate([high, high, low, low], 0)


def dual_of(target):
    return jnp.clip(target * RATIO, -BOUND, BOUND)


def levels(tau_ref):
    quantile = tau_ref[0].astype(F32) / QUANT
    return (quantile - 1.0) / penalty_fit, quantile / penalty_fit


def iterate(
    image_hbm, covs_ref, mask_ref, tau_ref,
    base_out, coef_out, split_out,
    image, dual, sums, partner, coefs, first_v, w_x, w_y, w_z, w_edge,
    edge_out, edge_in, gram_out, gram_in, covs_t,
    load_sem, sum_send, sum_recv, x_send, x_recv, y_send, y_recv, gram_send, gram_recv,
):
    part = lax.axis_index("sub")
    place = lax.axis_index("vox")
    pencils = lax.axis_size("vox")
    mate = (1 - part, place)
    right_x = (part, lax.rem(place + NPY, pencils))
    left_x = (part, lax.rem(place + pencils - NPY, pencils))
    right_y = (part, lax.rem(place + 1, pencils))
    left_y = (part, lax.rem(place + pencils - 1, pencils))
    pencil_y = lax.rem(lax.rem(place + NPY // 2, pencils), NPY)

    barrier = pltpu.get_barrier_semaphore()
    for device in (mate, right_x, left_x, right_y, left_y):
        pl.semaphore_signal(barrier, inc=1, device_id=device, device_id_type=MESH)

    def load(x):
        return pltpu.make_async_copy(
            image_hbm.at[:, pl.ds(pl.multiple_of(x * LAYER, LAYER), LAYER)],
            image.at[x], load_sem.at[x],
        )

    def send_sum(step, x):
        return pltpu.make_async_remote_copy(
            src_ref=sums.at[step, x], dst_ref=partner.at[step, x],
            send_sem=sum_send.at[step, x], recv_sem=sum_recv.at[step, x],
            device_id=mate, device_id_type=MESH,
        )

    def send_x(step, way):
        source, target, device = ((1, PX + 1, left_x), (PX, 0, right_x))[way]
        return pltpu.make_async_remote_copy(
            src_ref=coefs.at[step, source], dst_ref=coefs.at[step, target],
            send_sem=x_send.at[step, way], recv_sem=x_recv.at[step, way],
            device_id=device, device_id_type=MESH,
        )

    def send_y(step, way, half):
        return pltpu.make_async_remote_copy(
            src_ref=edge_out.at[step, way, half], dst_ref=edge_in.at[step, way, half],
            send_sem=y_send.at[step, way, half], recv_sem=y_recv.at[step, way, half],
            device_id=(left_y, right_y)[way], device_id_type=MESH,
        )

    send_gram = pltpu.make_async_remote_copy(
        src_ref=gram_out, dst_ref=gram_in, send_sem=gram_send, recv_sem=gram_recv,
        device_id=mate, device_id_type=MESH,
    )

    for x in range(PX):
        load(x).start()

    turned = covs_ref[...]
    high, low = halves(turned)
    covs_t[...] = jnp.concatenate([high, low], 0)
    pair = jnp.concatenate([high.astype(F32), low.astype(F32)], 0).T.astype(BF16)
    split_out[...] = jnp.concatenate([pair, pair], 1)
    gram_out[...] = lax.dot_general(
        turned, turned, (((1,), (1,)), ((), ())),
        precision=lax.Precision.HIGHEST, preferred_element_type=F32,
    )
    edge_out[...] = jnp.zeros_like(edge_out)

    floor, ceiling = levels(tau_ref)
    lane = lax.broadcasted_iota(jnp.int32, (COVARS, LAYER), 1)
    short = lax.broadcasted_iota(jnp.int32, (COVARS, 128), 1)
    valid_y = ((lane < LAYER - GZ) | (pencil_y < NPY - 1)).astype(F32)
    valid_z = (lax.rem(lane, GZ) < GZ - 1).astype(F32)
    has_left = ((short < GZ) & (pencil_y > 0)).astype(F32)

    def mask_of(x):
        return mask_ref[:, pl.ds(pl.multiple_of(x * LAYER, LAYER), LAYER)].astype(F32)

    def add_up(total, rows, high, low):
        both = product(covs_t[:, rows], high)
        one = product(covs_t[0:COVARS, rows], low)
        term = both[0:COVARS] + both[COVARS:] + one
        return term if total is None else total + term

    def first(x, carry):
        load(x).wait()
        total = None
        for block in range(image.shape[1] // ROWS):
            rows = slice(block * ROWS, (block + 1) * ROWS)
            total = add_up(total, rows, *halves(image[x, rows, :]))
        sums[0, x] = total * mask_of(x)
        send_sum(0, x).start()
        return carry

    pl.semaphore_wait(barrier, 5)
    send_gram.start()
    lax.fori_loop(0, PX, first, 0)

    send_gram.wait()
    gram = gram_out[...] + gram_in[...]
    row_bound = jnp.max(jnp.sum(jnp.abs(gram), axis=1, keepdims=True), axis=0, keepdims=True)
    eta = 1.0 / (penalty_fit * row_bound + 12.0 * penalty_tv)

    def pass_on(step, x, coef):
        coefs[step, x + 1] = coef
        quarter = lax.rem(x, 4)
        half = lax.div(x, 4)
        here = lax.div(short, GZ) == quarter
        front = pltpu.roll(coef[:, 0:128], quarter * GZ, 1)
        back = pltpu.roll(coef[:, 128:256], lax.rem(quarter * GZ + GZ, 128), 1)
        edge_out[step, 0, half] = jnp.where(here, front, edge_out[step, 0, half])
        edge_out[step, 1, half] = jnp.where(here, back, edge_out[step, 1, half])

        @pl.when(x == 0)
        def _():
            send_x(step, 0).start()

        @pl.when(x == PX - 1)
        def _():
            send_x(step, 1).start()

        for part_of in range(2):
            @pl.when(x == 4 * part_of + 3)
            def _():
                send_y(step, 0, part_of).start()
                send_y(step, 1, part_of).start()

    def residual(step, x, coef):
        right = stacked(coef)
        total = None
        for block in range(image.shape[1] // ROWS):
            rows = slice(block * ROWS, (block + 1) * ROWS)
            seen = image[x, rows, :]
            target = seen - product(split_out[rows, :], right)
            if step == 1:
                target = target + dual[x, rows, :]
            new = jnp.clip(target, floor, ceiling)
            if step == 0:
                dual[x, rows, :] = new
            else:
                base_out[x, rows, :] = seen + new
            total = add_up(total, rows, *halves(new))
        sums[step + 1, x] = total * mask_of(x)
        send_sum(step + 1, x).start()

    def smooth(step, x):
        for part_of in range(2):
            @pl.when(x == 4 * part_of)
            def _():
                send_y(step, 0, part_of).wait_recv()
                send_y(step, 1, part_of).wait_recv()

        @pl.when(x == 0)
        def _():
            send_x(step, 1).wait_recv()
            rise = coefs[step, 1] - coefs[step, 0]
            if step == 1:
                rise = rise + w_x[0]
            w_x[0] = dual_of(rise)

        @pl.when(x == PX - 1)
        def _():
            send_x(step, 0).wait_recv()

        quarter = lax.rem(x, 4)
        half = lax.div(x, 4)
        here = coefs[step, x + 1]
        rise_x = coefs[step, x + 2] - here
        after = pltpu.roll(edge_in[step, 0, half], (128 - GZ) - quarter * GZ, 1)
        before = pltpu.roll(edge_in[step, 1, half], lax.rem(128 - quarter * GZ, 128), 1)
        turned_y = pltpu.roll(here, LAYER - GZ, 1)
        next_y = jnp.concatenate(
            [turned_y[:, 0:128], jnp.where(short >= 128 - GZ, after, turned_y[:, 128:256])], 1
        )
        rise_y = valid_y * (next_y - here)
        rise_z = valid_z * (pltpu.roll(here, LAYER - 1, 1) - here)
        rise_edge = has_left * (here[:, 0:128] - before)
        if step == 1:
            rise_x = rise_x + w_x[x + 1]
            rise_y = rise_y + w_y[x]
            rise_z = rise_z + w_z[x]
            rise_edge = rise_edge + w_edge[x]
        new_x, new_y, new_z, new_edge = (dual_of(rise) for rise in (rise_x, rise_y, rise_z, rise_edge))
        summed = w_x[x] - new_x
        turned_y = pltpu.roll(new_y, GZ, 1)
        prev_y = jnp.concatenate(
            [jnp.where(short < GZ, new_edge, turned_y[:, 0:128]), turned_y[:, 128:256]], 1
        )
        summed = summed + (prev_y - new_y)
        summed = summed + (pltpu.roll(new_z, 1, 1) - new_z)
        w_x[x + 1] = new_x
        if step == 0:
            w_y[x] = new_y
            w_z[x] = new_z
            w_edge[x] = new_edge
        return summed

    def second(x, carry):
        send_sum(0, x).wait_recv()
        coef = eta * (sums[0, x] + partner[0, x])
        pass_on(0, x, coef)
        residual(0, x, coef)
        return carry

    def third(x, carry):
        summed = smooth(0, x)
        send_sum(1, x).wait_recv()
        change = (sums[1, x] + partner[1, x]) - summed
        first_v[x] = change
        coef = coefs[0, x + 1] + eta * (2.0 * change)
        pass_on(1, x, coef)
        residual(1, x, coef)
        return carry

    def last(x, carry):
        summed = smooth(1, x)
        send_sum(2, x).wait_recv()
        change = (sums[2, x] + partner[2, x]) - summed
        coef_out[x] = coefs[1, x + 1] + eta * (2.0 * change - first_v[x])
        return carry

    lax.fori_loop(0, PX, second, 0)
    lax.fori_loop(0, PX, third, 0)
    lax.fori_loop(0, PX, last, 0)

    for step in range(3):
        for x in range(PX):
            send_sum(step, x).wait_send()
    for step in range(2):
        for way in range(2):
            send_x(step, way).wait_send()
            for half in range(2):
                send_y(step, way, half).wait_send()


def finish(base, coef_ref, split_ref, mask_ref, tau_ref, coef_out, residual_out, result, out_sem, coef_sem):
    floor, ceiling = levels(tau_ref)

    def columns(x):
        return pl.ds(pl.multiple_of(x * LAYER, LAYER), LAYER)

    def put(x):
        return pltpu.make_async_copy(result.at[x], residual_out.at[:, columns(x)], out_sem.at[x])

    def put_coef(x):
        return pltpu.make_async_copy(coef_ref.at[x], coef_out.at[:, columns(x)], coef_sem.at[x])

    for x in range(PX):
        put_coef(x).start()

    def layer(x, carry):
        right = stacked(coef_ref[x])
        mask = mask_ref[:, columns(x)].astype(F32)
        for block in range(result.shape[1] // ROWS):
            rows = slice(block * ROWS, (block + 1) * ROWS)
            target = base[x, rows, :] - product(split_ref[rows, :], right)
            result[x, rows, :] = mask * (target - jnp.clip(target, floor, ceiling))
        put(x).start()
        return carry

    lax.fori_loop(0, PX, layer, 0)
    for x in range(PX):
        put_coef(x).wait()
        put(x).wait()


def per_device(observed, covariates, voxel_mask, tau_index):
    subjects, voxels = observed.shape
    mask = voxel_mask.reshape(1, voxels)
    vmem = pl.BlockSpec(memory_space=pltpu.VMEM)
    smem = pl.BlockSpec(memory_space=pltpu.SMEM)
    hbm = pl.BlockSpec(memory_space=pl.ANY)
    dma = pltpu.SemaphoreType.DMA
    base, coef, split = pl.pallas_call(
        iterate,
        out_shape=(
            pltpu.VMEM((PX, subjects, LAYER), F32),
            pltpu.VMEM((PX, COVARS, LAYER), F32),
            pltpu.VMEM((subjects, 4 * COVARS), BF16),
        ),
        in_specs=[hbm, vmem, vmem, smem],
        out_specs=(vmem, vmem, vmem),
        scratch_shapes=[
            pltpu.VMEM((PX, subjects, LAYER), F32),
            pltpu.VMEM((PX, subjects, LAYER), F32),
            pltpu.VMEM((3, PX, COVARS, LAYER), F32),
            pltpu.VMEM((3, PX, COVARS, LAYER), F32),
            pltpu.VMEM((2, PX + 2, COVARS, LAYER), F32),
            pltpu.VMEM((PX, COVARS, LAYER), F32),
            pltpu.VMEM((PX + 1, COVARS, LAYER), F32),
            pltpu.VMEM((PX, COVARS, LAYER), F32),
            pltpu.VMEM((PX, COVARS, LAYER), F32),
            pltpu.VMEM((PX, COVARS, 128), F32),
            pltpu.VMEM((2, 2, 2, COVARS, 128), F32),
            pltpu.VMEM((2, 2, 2, COVARS, 128), F32),
            pltpu.VMEM((COVARS, COVARS), F32),
            pltpu.VMEM((COVARS, COVARS), F32),
            pltpu.VMEM((2 * COVARS, subjects), BF16),
            dma((PX,)), dma((3, PX)), dma((3, PX)), dma((2, 2)), dma((2, 2)),
            dma((2, 2, 2)), dma((2, 2, 2)), dma, dma,
        ],
        compiler_params=pltpu.CompilerParams(
            collective_id=0, has_side_effects=True, vmem_limit_bytes=40 << 20
        ),
        name="iterate",
    )(observed, covariates.T, mask, tau_index)
    return pl.pallas_call(
        finish,
        out_shape=(
            jax.ShapeDtypeStruct((COVARS, voxels), F32),
            jax.ShapeDtypeStruct((subjects, voxels), F32),
        ),
        in_specs=[vmem, vmem, vmem, vmem, smem],
        out_specs=(hbm, hbm),
        scratch_shapes=[pltpu.VMEM((PX, subjects, LAYER), F32), dma((PX,)), dma((PX,))],
        compiler_params=pltpu.CompilerParams(vmem_limit_bytes=24 << 20),
        name="finish",
    )(base, coef, split, mask, tau_index)


def solution(mesh):
    return jax.shard_map(
        per_device,
        mesh=mesh,
        in_specs=(P("sub", "vox"), P("sub", None), P("vox"), P()),
        out_specs=(P(None, "vox"), P("sub", "vox")),
        check_vma=False,
    )
```

```python
import functools

import jax
import jax.numpy as jnp
from jax import lax
from jax.experimental import pallas as pl
from jax.experimental.pallas import tpu as pltpu
from jax.sharding import PartitionSpec as P

COVARS = 64
PX = 8
PY = 8
GZ = 32
NPY = 8
QUANT = 20
LAYER = PY * GZ
ROWS = 256
WINDOW = 2

penalty_fit = 1.0
penalty_tv = 1.0
tv_weight = 0.05
huber_width = 0.02
BOUND = tv_weight / penalty_tv
RATIO = BOUND / (huber_width + BOUND)

MESH = pl.DeviceIdType.MESH
F32 = jnp.float32
BF16 = jnp.bfloat16


def halves(value):
    high = value.astype(BF16)
    return high, (value - high.astype(F32)).astype(BF16)


def product(left, right):
    return jnp.dot(left, right, preferred_element_type=F32)


def stacked(coef):
    high, low = halves(coef)
    return jnp.concatenate([high, high, low, low], 0)


def dual_of(target):
    return jnp.clip(target * RATIO, -BOUND, BOUND)


def levels(tau_ref):
    quantile = tau_ref[0].astype(F32) / QUANT
    return (quantile - 1.0) / penalty_fit, quantile / penalty_fit


def iterate(
    image_hbm, covs_hbm, mask_hbm, tau_ref,
    base_out, coef_out, split_out, mask_out, level_out,
    image, dual, sums, partner, coefs, first_v, w_x, w_y, w_z, w_edge,
    edge_out, edge_in, gram_out, gram_in, covs_t, covs_ref, mask_ref,
    load_sem, covs_sem, mask_sem, sum_send, sum_recv, x_send, x_recv, y_send, y_recv, gram_send, gram_recv,
):
    part = lax.axis_index("sub")
    place = lax.axis_index("vox")
    pencils = lax.axis_size("vox")
    mate = (1 - part, place)
    right_x = (part, lax.rem(place + NPY, pencils))
    left_x = (part, lax.rem(place + pencils - NPY, pencils))
    right_y = (part, lax.rem(place + 1, pencils))
    left_y = (part, lax.rem(place + pencils - 1, pencils))
    crosses = lax.rem(place, 2)
    far_y = (lax.rem(part + crosses, 2), right_y[1])
    behind_y = (lax.rem(part + 1 - crosses, 2), left_y[1])
    pencil_y = lax.rem(lax.rem(place + NPY // 2, pencils), NPY)

    barrier = pltpu.get_barrier_semaphore()
    for device in (mate, right_x, left_x, right_y, behind_y):
        pl.semaphore_signal(barrier, inc=1, device_id=device, device_id_type=MESH)

    def layer_at(turn):
        return lax.rem(turn + PX - 1, PX)

    def load(x):
        return pltpu.make_async_copy(
            image_hbm.at[:, pl.ds(pl.multiple_of(x * LAYER, LAYER), LAYER)],
            image.at[x], load_sem.at[x],
        )

    def send_sum(number):
        return pltpu.make_async_remote_copy(
            src_ref=sums.at[number], dst_ref=partner.at[number],
            send_sem=sum_send.at[number], recv_sem=sum_recv.at[number],
            device_id=mate, device_id_type=MESH,
        )

    def give_sum(number):
        @pl.when(number >= WINDOW)
        def _():
            send_sum(number - WINDOW).wait_send()

        send_sum(number).start()

    def send_x(step, way):
        source, target, device = ((1, PX + 1, left_x), (PX, 0, right_x))[way]
        return pltpu.make_async_remote_copy(
            src_ref=coefs.at[step, source], dst_ref=coefs.at[step, target],
            send_sem=x_send.at[step, way], recv_sem=x_recv.at[step, way],
            device_id=device, device_id_type=MESH,
        )

    def send_y(step, way, x):
        return pltpu.make_async_remote_copy(
            src_ref=edge_out.at[step, way, x], dst_ref=edge_in.at[step, way, x],
            send_sem=y_send.at[step, way, x], recv_sem=y_recv.at[step, way, x],
            device_id=(left_y, far_y)[way], device_id_type=MESH,
        )

    send_gram = pltpu.make_async_remote_copy(
        src_ref=gram_out, dst_ref=gram_in, send_sem=gram_send, recv_sem=gram_recv,
        device_id=mate, device_id_type=MESH,
    )

    load_covs = pltpu.make_async_copy(covs_hbm, covs_ref, covs_sem)
    load_mask = pltpu.make_async_copy(mask_hbm, mask_ref, mask_sem)
    load_covs.start()
    load_mask.start()
    for turn in range(2):
        load(layer_at(turn)).start()

    load_covs.wait()
    covs = covs_ref[...]
    high, low = halves(covs)
    covs_t[...] = jnp.concatenate([high, low], 0)
    load_mask.wait()
    mask_out[...] = mask_ref[...].astype(F32)

    lane = lax.broadcasted_iota(jnp.int32, (COVARS, LAYER), 1)
    short = lax.broadcasted_iota(jnp.int32, (COVARS, 128), 1)
    valid_y = ((lane < LAYER - GZ) | (pencil_y < NPY - 1)).astype(F32)
    valid_z = (lax.rem(lane, GZ) < GZ - 1).astype(F32)
    has_left = ((short < GZ) & (pencil_y > 0)).astype(F32)

    def mask_of(x):
        return mask_out[:, pl.ds(pl.multiple_of(x * LAYER, LAYER), LAYER)]

    def packed(block):
        rows = COVARS // 4
        result = block[0:rows]
        for group in range(1, 4):
            moved = pltpu.roll(block[group * rows : (group + 1) * rows], group * GZ, 1)
            result = jnp.where(lax.div(short[0:rows], GZ) == group, moved, result)
        return result

    def unpacked(block, lane_at):
        moved = [(lane_at - group * GZ) % 128 for group in range(4)]
        return jnp.concatenate([pltpu.roll(block, by, 1) if by else block for by in moved], 0)

    def add_up(total, rows, high, low):
        both = product(covs_t[:, rows], high)
        one = product(covs_t[0:COVARS, rows], low)
        term = both[0:COVARS] + both[COVARS:] + one
        return term if total is None else total + term

    def first(turn, carry):
        x = layer_at(turn)
        load(x).wait()

        @pl.when(turn + 2 < PX)
        def _():
            load(layer_at(turn + 2)).start()

        total = None
        for block in range(image.shape[1] // ROWS):
            rows = slice(block * ROWS, (block + 1) * ROWS)
            total = add_up(total, rows, *halves(image[x, rows, :]))
        sums[turn] = total * mask_of(x)

        @pl.when(turn == 0)
        def _():
            pl.semaphore_wait(barrier, 5)

        give_sum(turn)

        @pl.when(turn == 0)
        def _():
            gram_out[...] = lax.dot_general(
                covs, covs, (((1,), (1,)), ((), ())),
                precision=lax.Precision.HIGHEST, preferred_element_type=F32,
            )
            send_gram.start()

        return carry

    lax.fori_loop(0, PX, first, 0)
    pair = jnp.concatenate([high.astype(F32), low.astype(F32)], 0).T.astype(BF16)
    split_out[...] = jnp.concatenate([pair, pair], 1)
    floor, ceiling = levels(tau_ref)
    level_out[0:1, :] = jnp.full((1, 128), floor, F32)
    level_out[1:2, :] = jnp.full((1, 128), ceiling, F32)

    send_gram.wait()
    gram = gram_out[...] + gram_in[...]
    row_bound = jnp.max(jnp.sum(jnp.abs(gram), axis=1, keepdims=True), axis=0, keepdims=True)
    eta = 1.0 / (penalty_fit * row_bound + 12.0 * penalty_tv)

    def pass_on(step, turn, x, coef):
        coefs[step, x + 1] = coef
        for way, block in ((0, coef[:, 0:128]), (1, pltpu.roll(coef[:, 128:256], GZ, 1))):
            edge_out[step, way, x] = packed(block)
            send_y(step, way, x).start()

        @pl.when(turn == 0)
        def _():
            send_x(step, 1).start()

        @pl.when(turn == 1)
        def _():
            send_x(step, 0).start()

    def residual(step, turn, x, coef):
        right = stacked(coef)
        total = None
        for block in range(image.shape[1] // ROWS):
            rows = slice(block * ROWS, (block + 1) * ROWS)
            seen = image[x, rows, :]
            target = seen - product(split_out[rows, :], right)
            if step == 1:
                target = target + dual[x, rows, :]
            new = jnp.clip(target, floor, ceiling)
            if step == 0:
                dual[x, rows, :] = new
            else:
                base_out[x, rows, :] = seen + new
            total = add_up(total, rows, *halves(new))
        number = (step + 1) * PX + turn
        sums[number] = total * mask_of(x)
        give_sum(number)

    def smooth(step, turn, x):
        def left_wall(at):
            rise = coefs[step, at + 1] - coefs[step, at]
            if step == 1:
                rise = rise + w_x[0, at]
            w_x[step, at] = dual_of(rise)

        @pl.when(turn == 0)
        def _():
            send_x(step, 0).wait_recv()
            left_wall(PX - 1)

        @pl.when(turn == 1)
        def _():
            send_x(step, 1).wait_recv()
            left_wall(0)

        send_y(step, 0, x).wait_recv()
        send_y(step, 1, x).wait_recv()
        here = coefs[step, x + 1]
        rise_x = coefs[step, x + 2] - here
        after = unpacked(edge_in[step, 0, x], 128 - GZ)
        before = unpacked(edge_in[step, 1, x], 0)
        turned_y = pltpu.roll(here, LAYER - GZ, 1)
        next_y = jnp.concatenate(
            [turned_y[:, 0:128], jnp.where(short >= 128 - GZ, after, turned_y[:, 128:256])], 1
        )
        rise_y = valid_y * (next_y - here)
        rise_z = valid_z * (pltpu.roll(here, LAYER - 1, 1) - here)
        rise_edge = has_left * (here[:, 0:128] - before)
        if step == 1:
            rise_x = rise_x + w_x[0, x + 1]
            rise_y = rise_y + w_y[x]
            rise_z = rise_z + w_z[x]
            rise_edge = rise_edge + w_edge[x]
        new_x, new_y, new_z, new_edge = (dual_of(rise) for rise in (rise_x, rise_y, rise_z, rise_edge))
        summed = w_x[step, x] - new_x
        turned_y = pltpu.roll(new_y, GZ, 1)
        prev_y = jnp.concatenate(
            [jnp.where(short < GZ, new_edge, turned_y[:, 0:128]), turned_y[:, 128:256]], 1
        )
        summed = summed + (prev_y - new_y)
        summed = summed + (pltpu.roll(new_z, 1, 1) - new_z)
        w_x[step, x + 1] = new_x
        if step == 0:
            w_y[x] = new_y
            w_z[x] = new_z
            w_edge[x] = new_edge
        return summed

    def total_of(number):
        send_sum(number).wait_recv()
        return sums[number] + partner[number]

    def second(turn, carry):
        x = layer_at(turn)
        coef = eta * total_of(turn)
        pass_on(0, turn, x, coef)
        residual(0, turn, x, coef)
        return carry

    def third(turn, carry):
        x = layer_at(turn)
        summed = smooth(0, turn, x)
        change = total_of(PX + turn) - summed
        first_v[x] = change
        coef = coefs[0, x + 1] + eta * (2.0 * change)
        pass_on(1, turn, x, coef)
        residual(1, turn, x, coef)
        return carry

    def last(turn, carry):
        x = layer_at(turn)
        summed = smooth(1, turn, x)
        change = total_of(2 * PX + turn) - summed
        coef_out[x] = coefs[1, x + 1] + eta * (2.0 * change - first_v[x])
        return carry

    lax.fori_loop(0, PX, second, 0)
    lax.fori_loop(0, PX, third, 0)
    lax.fori_loop(0, PX, last, 0)

    for number in range(3 * PX - WINDOW, 3 * PX):
        send_sum(number).wait_send()
    for step in range(2):
        for way in range(2):
            send_x(step, way).wait_send()
            for x in range(PX):
                send_y(step, way, x).wait_send()


def finish(base, coef_ref, split_ref, mask_ref, level_ref, coef_out, residual_out, result, out_sem, coef_sem):
    floor, ceiling = level_ref[0:1, 0:1], level_ref[1:2, 0:1]

    def columns(x):
        return pl.ds(pl.multiple_of(x * LAYER, LAYER), LAYER)

    def put(x):
        return pltpu.make_async_copy(result.at[x], residual_out.at[:, columns(x)], out_sem.at[x])

    def put_coef(x):
        return pltpu.make_async_copy(coef_ref.at[x], coef_out.at[:, columns(x)], coef_sem.at[x])

    for x in range(PX):
        put_coef(x).start()

    def layer(x, carry):
        right = stacked(coef_ref[x])
        mask = mask_ref[:, columns(x)]
        for block in range(result.shape[1] // ROWS):
            rows = slice(block * ROWS, (block + 1) * ROWS)
            target = base[x, rows, :] - product(split_ref[rows, :], right)
            result[x, rows, :] = mask * (target - jnp.clip(target, floor, ceiling))
        put(x).start()
        return carry

    lax.fori_loop(0, PX, layer, 0)
    for x in range(PX):
        put_coef(x).wait()
        put(x).wait()


def per_device(observed, covariates, voxel_mask, tau_index):
    subjects, voxels = observed.shape
    inputs = [
        pltpu.with_memory_space_constraint(value, pltpu.HBM)
        for value in (observed, covariates.T, voxel_mask.reshape(1, voxels))
    ]
    vmem = pl.BlockSpec(memory_space=pltpu.VMEM)
    smem = pl.BlockSpec(memory_space=pltpu.SMEM)
    hbm = pl.BlockSpec(memory_space=pltpu.HBM)
    dma = pltpu.SemaphoreType.DMA
    made = pl.pallas_call(
        iterate,
        out_shape=(
            pltpu.VMEM((PX, subjects, LAYER), F32),
            pltpu.VMEM((PX, COVARS, LAYER), F32),
            pltpu.VMEM((subjects, 4 * COVARS), BF16),
            pltpu.VMEM((1, voxels), F32),
            pltpu.VMEM((2, 128), F32),
        ),
        in_specs=[hbm, hbm, hbm, smem],
        out_specs=(vmem,) * 5,
        scratch_shapes=[
            pltpu.VMEM((PX, subjects, LAYER), F32),
            pltpu.VMEM((PX, subjects, LAYER), F32),
            pltpu.VMEM((3 * PX, COVARS, LAYER), F32),
            pltpu.VMEM((3 * PX, COVARS, LAYER), F32),
            pltpu.VMEM((2, PX + 2, COVARS, LAYER), F32),
            pltpu.VMEM((PX, COVARS, LAYER), F32),
            pltpu.VMEM((2, PX + 1, COVARS, LAYER), F32),
            pltpu.VMEM((PX, COVARS, LAYER), F32),
            pltpu.VMEM((PX, COVARS, LAYER), F32),
            pltpu.VMEM((PX, COVARS, 128), F32),
            pltpu.VMEM((2, 2, PX, COVARS // 4, 128), F32),
            pltpu.VMEM((2, 2, PX, COVARS // 4, 128), F32),
            pltpu.VMEM((COVARS, COVARS), F32),
            pltpu.VMEM((COVARS, COVARS), F32),
            pltpu.VMEM((2 * COVARS, subjects), BF16),
            pltpu.VMEM((COVARS, subjects), F32),
            pltpu.VMEM((1, voxels), jnp.int32),
            dma((PX,)), dma, dma, dma((3 * PX,)), dma((3 * PX,)), dma((2, 2)), dma((2, 2)),
            dma((2, 2, PX)), dma((2, 2, PX)), dma, dma,
        ],
        compiler_params=pltpu.CompilerParams(
            collective_id=0, has_side_effects=True, vmem_limit_bytes=40 << 20
        ),
        name="iterate",
    )(*inputs, tau_index)
    return pl.pallas_call(
        finish,
        out_shape=(
            jax.ShapeDtypeStruct((COVARS, voxels), F32),
            jax.ShapeDtypeStruct((subjects, voxels), F32),
        ),
        in_specs=[vmem] * 5,
        out_specs=(hbm, hbm),
        scratch_shapes=[pltpu.VMEM((PX, subjects, LAYER), F32), dma((PX,)), dma((PX,))],
        compiler_params=pltpu.CompilerParams(vmem_limit_bytes=24 << 20),
        name="finish",
    )(*made)


def solution(mesh):
    return jax.shard_map(
        per_device,
        mesh=mesh,
        in_specs=(P("sub", "vox"), P("sub", None), P("vox"), P()),
        out_specs=(P(None, "vox"), P("sub", "vox")),
        check_vma=False,
    )
```

```python
import functools

import jax
import jax.numpy as jnp
from jax import lax
from jax.experimental import pallas as pl
from jax.experimental.pallas import tpu as pltpu
from jax.sharding import PartitionSpec as P

COVARS = 64
PX = 8
PY = 8
GZ = 32
NPY = 8
QUANT = 20
LAYER = PY * GZ
ROWS = 256
WINDOW = 4

penalty_fit = 1.0
penalty_tv = 1.0
tv_weight = 0.05
huber_width = 0.02
BOUND = tv_weight / penalty_tv
RATIO = BOUND / (huber_width + BOUND)

MESH = pl.DeviceIdType.MESH
F32 = jnp.float32
BF16 = jnp.bfloat16


def halves(value):
    high = value.astype(BF16)
    return high, (value - high.astype(F32)).astype(BF16)


def product(left, right):
    return jnp.dot(left, right, preferred_element_type=F32)


def stacked(coef):
    high, low = halves(coef)
    return jnp.concatenate([high, high, low, low], 0)


def dual_of(target):
    return jnp.clip(target * RATIO, -BOUND, BOUND)


def levels(tau_ref):
    quantile = tau_ref[0].astype(F32) / QUANT
    return (quantile - 1.0) / penalty_fit, quantile / penalty_fit


def iterate(
    image_hbm, covs_hbm, mask_hbm, tau_ref,
    base_out, coef_out, split_out, mask_out, level_out,
    image, dual, sums, partner, coefs, first_v, w_x, w_y, w_z, w_edge,
    edge_out, edge_in, gram_out, gram_in, covs_t, covs_ref, mask_ref,
    load_sem, covs_sem, mask_sem, sum_send, sum_recv, x_send, x_recv, y_send, y_recv, gram_send, gram_recv, mate_in, all_in,
):
    part = lax.axis_index("sub")
    place = lax.axis_index("vox")
    pencils = lax.axis_size("vox")
    mate = (1 - part, place)
    right_x = (part, lax.rem(place + NPY, pencils))
    left_x = (part, lax.rem(place + pencils - NPY, pencils))
    right_y = (part, lax.rem(place + 1, pencils))
    left_y = (part, lax.rem(place + pencils - 1, pencils))
    crosses = lax.rem(place, 2)
    far_y = (lax.rem(part + crosses, 2), right_y[1])
    behind_y = (lax.rem(part + 1 - crosses, 2), left_y[1])
    pencil_y = lax.rem(lax.rem(place + NPY // 2, pencils), NPY)

    barrier = pltpu.get_barrier_semaphore()

    def signal(semaphore, device):
        pl.semaphore_signal(semaphore, inc=1, device_id=device, device_id_type=MESH)

    @pl.when(part == 0)
    def _():
        signal(barrier, mate)

    def layer_at(turn):
        return lax.rem(turn + PX - 1, PX)

    def load(x):
        return pltpu.make_async_copy(
            image_hbm.at[:, pl.ds(pl.multiple_of(x * LAYER, LAYER), LAYER)],
            image.at[x], load_sem.at[x],
        )

    def send_sum(number):
        return pltpu.make_async_remote_copy(
            src_ref=sums.at[number], dst_ref=partner.at[number],
            send_sem=sum_send.at[number], recv_sem=sum_recv.at[number],
            device_id=mate, device_id_type=MESH,
        )

    def give_sum(number):
        @pl.when(number >= WINDOW)
        def _():
            send_sum(number - WINDOW).wait_send()

        send_sum(number).start()

    def send_x(step, way):
        source, target, device = ((1, PX + 1, left_x), (PX, 0, right_x))[way]
        return pltpu.make_async_remote_copy(
            src_ref=coefs.at[step, source], dst_ref=coefs.at[step, target],
            send_sem=x_send.at[step, way], recv_sem=x_recv.at[step, way],
            device_id=device, device_id_type=MESH,
        )

    def send_y(step, way, x):
        return pltpu.make_async_remote_copy(
            src_ref=edge_out.at[step, way, x], dst_ref=edge_in.at[step, way, x],
            send_sem=y_send.at[step, way, x], recv_sem=y_recv.at[step, way, x],
            device_id=(left_y, far_y)[way], device_id_type=MESH,
        )

    send_gram = pltpu.make_async_remote_copy(
        src_ref=gram_out, dst_ref=gram_in, send_sem=gram_send, recv_sem=gram_recv,
        device_id=mate, device_id_type=MESH,
    )

    load_covs = pltpu.make_async_copy(covs_hbm, covs_ref, covs_sem)
    load_mask = pltpu.make_async_copy(mask_hbm, mask_ref, mask_sem)
    load_covs.start()
    load_mask.start()
    for turn in range(2):
        load(layer_at(turn)).start()

    @pl.when(part == 1)
    def _():
        pl.semaphore_wait(barrier, 1)
        signal(mate_in, mate)

    load_covs.wait()
    covs = covs_ref[...]
    high, low = halves(covs)
    covs_t[...] = jnp.concatenate([high, low], 0)
    load_mask.wait()
    mask_out[...] = mask_ref[...].astype(F32)

    lane = lax.broadcasted_iota(jnp.int32, (COVARS, LAYER), 1)
    short = lax.broadcasted_iota(jnp.int32, (COVARS, 128), 1)
    valid_y = ((lane < LAYER - GZ) | (pencil_y < NPY - 1)).astype(F32)
    valid_z = (lax.rem(lane, GZ) < GZ - 1).astype(F32)
    has_left = ((short < GZ) & (pencil_y > 0)).astype(F32)

    def mask_of(x):
        return mask_out[:, pl.ds(pl.multiple_of(x * LAYER, LAYER), LAYER)]

    def packed(block):
        rows = COVARS // 4
        result = block[0:rows]
        for group in range(1, 4):
            moved = pltpu.roll(block[group * rows : (group + 1) * rows], group * GZ, 1)
            result = jnp.where(lax.div(short[0:rows], GZ) == group, moved, result)
        return result

    def unpacked(block, lane_at):
        moved = [(lane_at - group * GZ) % 128 for group in range(4)]
        return jnp.concatenate([pltpu.roll(block, by, 1) if by else block for by in moved], 0)

    def add_up(total, rows, high, low):
        both = product(covs_t[:, rows], high)
        one = product(covs_t[0:COVARS, rows], low)
        term = both[0:COVARS] + both[COVARS:] + one
        return term if total is None else total + term

    def first(turn, carry):
        x = layer_at(turn)
        load(x).wait()

        @pl.when(turn + 2 < PX)
        def _():
            load(layer_at(turn + 2)).start()

        total = None
        for block in range(image.shape[1] // ROWS):
            rows = slice(block * ROWS, (block + 1) * ROWS)
            total = add_up(total, rows, *halves(image[x, rows, :]))
        sums[turn] = total * mask_of(x)

        @pl.when((turn == 0) & (part == 0))
        def _():
            pl.semaphore_wait(mate_in, 1)
            for device in (right_x, left_x, right_y, left_y):
                signal(barrier, device)

        give_sum(turn)

        @pl.when(turn == 0)
        def _():
            gram_out[...] = lax.dot_general(
                covs, covs, (((1,), (1,)), ((), ())),
                precision=lax.Precision.HIGHEST, preferred_element_type=F32,
            )
            send_gram.start()

        return carry

    lax.fori_loop(0, PX, first, 0)
    pair = jnp.concatenate([high.astype(F32), low.astype(F32)], 0).T.astype(BF16)
    split_out[...] = jnp.concatenate([pair, pair], 1)
    floor, ceiling = levels(tau_ref)
    level_out[0:1, :] = jnp.full((1, 128), floor, F32)
    level_out[1:2, :] = jnp.full((1, 128), ceiling, F32)

    send_gram.wait()
    gram = gram_out[...] + gram_in[...]
    row_bound = jnp.max(jnp.sum(jnp.abs(gram), axis=1, keepdims=True), axis=0, keepdims=True)
    eta = 1.0 / (penalty_fit * row_bound + 12.0 * penalty_tv)

    def pass_on(step, turn, x, coef):
        coefs[step, x + 1] = coef
        for way, block in ((0, coef[:, 0:128]), (1, pltpu.roll(coef[:, 128:256], GZ, 1))):
            edge_out[step, way, x] = packed(block)
            send_y(step, way, x).start()

        @pl.when(turn == 0)
        def _():
            send_x(step, 1).start()

        @pl.when(turn == 1)
        def _():
            send_x(step, 0).start()

    def residual(step, turn, x, coef):
        right = stacked(coef)
        total = None
        for block in range(image.shape[1] // ROWS):
            rows = slice(block * ROWS, (block + 1) * ROWS)
            seen = image[x, rows, :]
            target = seen - product(split_out[rows, :], right)
            if step == 1:
                target = target + dual[x, rows, :]
            new = jnp.clip(target, floor, ceiling)
            if step == 0:
                dual[x, rows, :] = new
            else:
                base_out[x, rows, :] = seen + new
            total = add_up(total, rows, *halves(new))
        number = (step + 1) * PX + turn
        sums[number] = total * mask_of(x)
        give_sum(number)

    def smooth(step, turn, x):
        def left_wall(at):
            rise = coefs[step, at + 1] - coefs[step, at]
            if step == 1:
                rise = rise + w_x[0, at]
            w_x[step, at] = dual_of(rise)

        @pl.when(turn == 0)
        def _():
            send_x(step, 0).wait_recv()
            left_wall(PX - 1)

        @pl.when(turn == 1)
        def _():
            send_x(step, 1).wait_recv()
            left_wall(0)

        send_y(step, 0, x).wait_recv()
        send_y(step, 1, x).wait_recv()
        here = coefs[step, x + 1]
        rise_x = coefs[step, x + 2] - here
        after = unpacked(edge_in[step, 0, x], 128 - GZ)
        before = unpacked(edge_in[step, 1, x], 0)
        turned_y = pltpu.roll(here, LAYER - GZ, 1)
        next_y = jnp.concatenate(
            [turned_y[:, 0:128], jnp.where(short >= 128 - GZ, after, turned_y[:, 128:256])], 1
        )
        rise_y = valid_y * (next_y - here)
        rise_z = valid_z * (pltpu.roll(here, LAYER - 1, 1) - here)
        rise_edge = has_left * (here[:, 0:128] - before)
        if step == 1:
            rise_x = rise_x + w_x[0, x + 1]
            rise_y = rise_y + w_y[x]
            rise_z = rise_z + w_z[x]
            rise_edge = rise_edge + w_edge[x]
        new_x, new_y, new_z, new_edge = (dual_of(rise) for rise in (rise_x, rise_y, rise_z, rise_edge))
        summed = w_x[step, x] - new_x
        turned_y = pltpu.roll(new_y, GZ, 1)
        prev_y = jnp.concatenate(
            [jnp.where(short < GZ, new_edge, turned_y[:, 0:128]), turned_y[:, 128:256]], 1
        )
        summed = summed + (prev_y - new_y)
        summed = summed + (pltpu.roll(new_z, 1, 1) - new_z)
        w_x[step, x + 1] = new_x
        if step == 0:
            w_y[x] = new_y
            w_z[x] = new_z
            w_edge[x] = new_edge
        return summed

    def total_of(number):
        send_sum(number).wait_recv()
        return sums[number] + partner[number]

    def second(turn, carry):
        x = layer_at(turn)
        coef = eta * total_of(turn)
        pass_on(0, turn, x, coef)
        residual(0, turn, x, coef)
        return carry

    def third(turn, carry):
        x = layer_at(turn)
        summed = smooth(0, turn, x)
        change = total_of(PX + turn) - summed
        first_v[x] = change
        coef = coefs[0, x + 1] + eta * (2.0 * change)
        pass_on(1, turn, x, coef)
        residual(1, turn, x, coef)
        return carry

    def last(turn, carry):
        x = layer_at(turn)
        summed = smooth(1, turn, x)
        change = total_of(2 * PX + turn) - summed
        coef_out[x] = coefs[1, x + 1] + eta * (2.0 * change - first_v[x])
        return carry

    @pl.when(part == 0)
    def _():
        pl.semaphore_wait(barrier, 4)
        signal(all_in, mate)

    @pl.when(part == 1)
    def _():
        pl.semaphore_wait(all_in, 1)

    lax.fori_loop(0, PX, second, 0)
    lax.fori_loop(0, PX, third, 0)
    lax.fori_loop(0, PX, last, 0)

    for number in range(3 * PX - WINDOW, 3 * PX):
        send_sum(number).wait_send()
    for step in range(2):
        for way in range(2):
            send_x(step, way).wait_send()
            for x in range(PX):
                send_y(step, way, x).wait_send()


def finish(base, coef_ref, split_ref, mask_ref, level_ref, coef_out, residual_out, result, out_sem, coef_sem):
    floor, ceiling = level_ref[0:1, 0:1], level_ref[1:2, 0:1]

    def columns(x):
        return pl.ds(pl.multiple_of(x * LAYER, LAYER), LAYER)

    def put(x):
        return pltpu.make_async_copy(result.at[x], residual_out.at[:, columns(x)], out_sem.at[x])

    def put_coef(x):
        return pltpu.make_async_copy(coef_ref.at[x], coef_out.at[:, columns(x)], coef_sem.at[x])

    for x in range(PX):
        put_coef(x).start()

    def layer(x, carry):
        right = stacked(coef_ref[x])
        mask = mask_ref[:, columns(x)]
        for block in range(result.shape[1] // ROWS):
            rows = slice(block * ROWS, (block + 1) * ROWS)
            target = base[x, rows, :] - product(split_ref[rows, :], right)
            result[x, rows, :] = mask * (target - jnp.clip(target, floor, ceiling))
        put(x).start()
        return carry

    lax.fori_loop(0, PX, layer, 0)
    for x in range(PX):
        put_coef(x).wait()
        put(x).wait()


def per_device(observed, covariates, voxel_mask, tau_index):
    subjects, voxels = observed.shape
    inputs = [
        pltpu.with_memory_space_constraint(value, pltpu.HBM)
        for value in (observed, covariates.T, voxel_mask.reshape(1, voxels))
    ]
    vmem = pl.BlockSpec(memory_space=pltpu.VMEM)
    smem = pl.BlockSpec(memory_space=pltpu.SMEM)
    hbm = pl.BlockSpec(memory_space=pltpu.HBM)
    dma = pltpu.SemaphoreType.DMA
    made = pl.pallas_call(
        iterate,
        out_shape=(
            pltpu.VMEM((PX, subjects, LAYER), F32),
            pltpu.VMEM((PX, COVARS, LAYER), F32),
            pltpu.VMEM((subjects, 4 * COVARS), BF16),
            pltpu.VMEM((1, voxels), F32),
            pltpu.VMEM((2, 128), F32),
        ),
        in_specs=[hbm, hbm, hbm, smem],
        out_specs=(vmem,) * 5,
        scratch_shapes=[
            pltpu.VMEM((PX, subjects, LAYER), F32),
            pltpu.VMEM((PX, subjects, LAYER), F32),
            pltpu.VMEM((3 * PX, COVARS, LAYER), F32),
            pltpu.VMEM((3 * PX, COVARS, LAYER), F32),
            pltpu.VMEM((2, PX + 2, COVARS, LAYER), F32),
            pltpu.VMEM((PX, COVARS, LAYER), F32),
            pltpu.VMEM((2, PX + 1, COVARS, LAYER), F32),
            pltpu.VMEM((PX, COVARS, LAYER), F32),
            pltpu.VMEM((PX, COVARS, LAYER), F32),
            pltpu.VMEM((PX, COVARS, 128), F32),
            pltpu.VMEM((2, 2, PX, COVARS // 4, 128), F32),
            pltpu.VMEM((2, 2, PX, COVARS // 4, 128), F32),
            pltpu.VMEM((COVARS, COVARS), F32),
            pltpu.VMEM((COVARS, COVARS), F32),
            pltpu.VMEM((2 * COVARS, subjects), BF16),
            pltpu.VMEM((COVARS, subjects), F32),
            pltpu.VMEM((1, voxels), jnp.int32),
            dma((PX,)), dma, dma, dma((3 * PX,)), dma((3 * PX,)), dma((2, 2)), dma((2, 2)),
            dma((2, 2, PX)), dma((2, 2, PX)), dma, dma,
            pltpu.SemaphoreType.REGULAR, pltpu.SemaphoreType.REGULAR,
        ],
        compiler_params=pltpu.CompilerParams(
            collective_id=0, has_side_effects=True, vmem_limit_bytes=40 << 20
        ),
        name="iterate",
    )(*inputs, tau_index)
    return pl.pallas_call(
        finish,
        out_shape=(
            jax.ShapeDtypeStruct((COVARS, voxels), F32),
            jax.ShapeDtypeStruct((subjects, voxels), F32),
        ),
        in_specs=[vmem] * 5,
        out_specs=(hbm, hbm),
        scratch_shapes=[pltpu.VMEM((PX, subjects, LAYER), F32), dma((PX,)), dma((PX,))],
        compiler_params=pltpu.CompilerParams(vmem_limit_bytes=24 << 20),
        name="finish",
    )(*made)


def solution(mesh):
    return jax.shard_map(
        per_device,
        mesh=mesh,
        in_specs=(P("sub", "vox"), P("sub", None), P("vox"), P()),
        out_specs=(P(None, "vox"), P("sub", "vox")),
        check_vma=False,
    )
```

```python
import functools

import jax
import jax.numpy as jnp
from jax import lax
from jax.experimental import pallas as pl
from jax.experimental.pallas import tpu as pltpu
from jax.sharding import PartitionSpec as P

COVARS = 64
PX = 8
PY = 8
GZ = 32
NPY = 8
QUANT = 20
LAYER = PY * GZ
ROWS = 256
WINDOW = 4

penalty_fit = 1.0
penalty_tv = 1.0
tv_weight = 0.05
huber_width = 0.02
BOUND = tv_weight / penalty_tv
RATIO = BOUND / (huber_width + BOUND)

MESH = pl.DeviceIdType.MESH
F32 = jnp.float32
BF16 = jnp.bfloat16


def halves(value):
    high = value.astype(BF16)
    return high, (value - high.astype(F32)).astype(BF16)


def product(left, right):
    return jnp.dot(left, right, preferred_element_type=F32)


def stacked(coef):
    high, low = halves(coef)
    return jnp.concatenate([high, high, low, low], 0)


def dual_of(target):
    return jnp.clip(target * RATIO, -BOUND, BOUND)


def levels(tau_ref):
    quantile = tau_ref[0].astype(F32) / QUANT
    return (quantile - 1.0) / penalty_fit, quantile / penalty_fit


def iterate(
    image_hbm, covs_hbm, mask_hbm, tau_ref,
    base_out, coef_out, split_out, mask_out, level_out,
    image, dual, sums, partner, coefs, first_v, w_x, w_y, w_z, w_edge,
    edge_out, edge_in, gram_out, gram_in, covs_t, covs_ref, mask_ref,
    load_sem, covs_sem, mask_sem, sum_send, sum_recv, x_send, x_recv, y_send, y_recv, gram_send, gram_recv, mate_in, all_in,
):
    part = lax.axis_index("sub")
    place = lax.axis_index("vox")
    pencils = lax.axis_size("vox")
    mate = (1 - part, place)
    right_x = (part, lax.rem(place + NPY, pencils))
    left_x = (part, lax.rem(place + pencils - NPY, pencils))
    right_y = (part, lax.rem(place + 1, pencils))
    left_y = (part, lax.rem(place + pencils - 1, pencils))
    crosses = lax.rem(place, 2)
    far_y = (lax.rem(part + crosses, 2), right_y[1])
    behind_y = (lax.rem(part + 1 - crosses, 2), left_y[1])
    pencil_y = lax.rem(lax.rem(place + NPY // 2, pencils), NPY)

    barrier = pltpu.get_barrier_semaphore()

    def signal(semaphore, device):
        pl.semaphore_signal(semaphore, inc=1, device_id=device, device_id_type=MESH)

    @pl.when(part == 0)
    def _():
        signal(barrier, mate)

    def layer_at(turn):
        return lax.rem(turn + PX - 1, PX)

    def load(x):
        return pltpu.make_async_copy(
            image_hbm.at[:, pl.ds(pl.multiple_of(x * LAYER, LAYER), LAYER)],
            image.at[x], load_sem.at[x],
        )

    def send_sum(number):
        return pltpu.make_async_remote_copy(
            src_ref=sums.at[number], dst_ref=partner.at[number],
            send_sem=sum_send.at[number], recv_sem=sum_recv.at[number],
            device_id=mate, device_id_type=MESH,
        )

    def give_sum(number):
        @pl.when(number >= WINDOW)
        def _():
            send_sum(number - WINDOW).wait_send()

        send_sum(number).start()

    def send_x(step, way):
        source, target, device = ((1, PX + 1, left_x), (PX, 0, right_x))[way]
        return pltpu.make_async_remote_copy(
            src_ref=coefs.at[step, source], dst_ref=coefs.at[step, target],
            send_sem=x_send.at[step, way], recv_sem=x_recv.at[step, way],
            device_id=device, device_id_type=MESH,
        )

    def send_y(step, way, x):
        return pltpu.make_async_remote_copy(
            src_ref=edge_out.at[step, way, x], dst_ref=edge_in.at[step, way, x],
            send_sem=y_send.at[step, way, x], recv_sem=y_recv.at[step, way, x],
            device_id=(left_y, far_y)[way], device_id_type=MESH,
        )

    send_gram = pltpu.make_async_remote_copy(
        src_ref=gram_out, dst_ref=gram_in, send_sem=gram_send, recv_sem=gram_recv,
        device_id=mate, device_id_type=MESH,
    )

    load_covs = pltpu.make_async_copy(covs_hbm, covs_ref, covs_sem)
    load_mask = pltpu.make_async_copy(mask_hbm, mask_ref, mask_sem)
    load_covs.start()
    load_mask.start()
    for turn in range(2):
        load(layer_at(turn)).start()

    @pl.when(part == 1)
    def _():
        pl.semaphore_wait(barrier, 1)
        signal(mate_in, mate)

    load_covs.wait()
    covs = covs_ref[...]
    high, low = halves(covs)
    covs_t[...] = jnp.concatenate([high, low], 0)
    load_mask.wait()
    mask_out[...] = mask_ref[...].astype(F32)

    lane = lax.broadcasted_iota(jnp.int32, (COVARS, LAYER), 1)
    short = lax.broadcasted_iota(jnp.int32, (COVARS, 128), 1)
    valid_y = ((lane < LAYER - GZ) | (pencil_y < NPY - 1)).astype(F32)
    valid_z = (lax.rem(lane, GZ) < GZ - 1).astype(F32)
    has_left = ((short < GZ) & (pencil_y > 0)).astype(F32)

    def mask_of(x):
        return mask_out[:, pl.ds(pl.multiple_of(x * LAYER, LAYER), LAYER)]

    def packed(block):
        rows = COVARS // 4
        result = block[0:rows]
        for group in range(1, 4):
            moved = pltpu.roll(block[group * rows : (group + 1) * rows], group * GZ, 1)
            result = jnp.where(lax.div(short[0:rows], GZ) == group, moved, result)
        return result

    def unpacked(block, lane_at):
        moved = [(lane_at - group * GZ) % 128 for group in range(4)]
        return jnp.concatenate([pltpu.roll(block, by, 1) if by else block for by in moved], 0)

    def add_up(total, rows, high, low):
        both = product(covs_t[:, rows], high)
        one = product(covs_t[0:COVARS, rows], low)
        term = both[0:COVARS] + both[COVARS:] + one
        return term if total is None else total + term

    def first(turn, carry):
        x = layer_at(turn)
        load(x).wait()

        @pl.when(turn + 2 < PX)
        def _():
            load(layer_at(turn + 2)).start()

        total = None
        for block in range(image.shape[1] // ROWS):
            rows = slice(block * ROWS, (block + 1) * ROWS)
            total = add_up(total, rows, *halves(image[x, rows, :]))
        sums[turn] = total * mask_of(x)

        @pl.when((turn == 0) & (part == 0))
        def _():
            pl.semaphore_wait(mate_in, 1)
            for device in (right_x, left_x, right_y, left_y):
                signal(barrier, device)

        give_sum(turn)

        @pl.when(turn == 0)
        def _():
            gram_out[...] = lax.dot_general(
                covs, covs, (((1,), (1,)), ((), ())),
                precision=lax.Precision.HIGHEST, preferred_element_type=F32,
            )
            send_gram.start()

        return carry

    lax.fori_loop(0, PX, first, 0)
    pair = jnp.concatenate([high.astype(F32), low.astype(F32)], 0).T.astype(BF16)
    split_out[...] = jnp.concatenate([pair, pair], 1)
    floor, ceiling = levels(tau_ref)
    level_out[0:1, :] = jnp.full((1, 128), floor, F32)
    level_out[1:2, :] = jnp.full((1, 128), ceiling, F32)

    send_gram.wait()
    gram = gram_out[...] + gram_in[...]
    row_bound = jnp.max(jnp.sum(jnp.abs(gram), axis=1, keepdims=True), axis=0, keepdims=True)
    eta = 1.0 / (penalty_fit * row_bound + 12.0 * penalty_tv)

    def pass_on(step, turn, x, coef):
        coefs[step, x + 1] = coef
        for way, block in ((0, coef[:, 0:128]), (1, pltpu.roll(coef[:, 128:256], GZ, 1))):
            edge_out[step, way, x] = packed(block)
            send_y(step, way, x).start()

        @pl.when(turn == 0)
        def _():
            send_x(step, 1).start()

        @pl.when(turn == 1)
        def _():
            send_x(step, 0).start()

    def residual(step, turn, x, coef):
        right = stacked(coef)
        total = None
        for block in range(image.shape[1] // ROWS):
            rows = slice(block * ROWS, (block + 1) * ROWS)
            seen = image[x, rows, :]
            target = seen - product(split_out[rows, :], right)
            if step == 1:
                target = target + dual[x, rows, :]
            new = jnp.clip(target, floor, ceiling)
            if step == 0:
                dual[x, rows, :] = new
            else:
                base_out[x, rows, :] = seen + new
            total = add_up(total, rows, *halves(new))
        number = (step + 1) * PX + turn
        sums[number] = total * mask_of(x)
        give_sum(number)

    def smooth(step, turn, x):
        def left_wall(at):
            rise = coefs[step, at + 1] - coefs[step, at]
            if step == 1:
                rise = rise + w_x[0, at]
            w_x[step, at] = dual_of(rise)

        @pl.when(turn == 0)
        def _():
            send_x(step, 0).wait_recv()
            left_wall(PX - 1)

        @pl.when(turn == 1)
        def _():
            send_x(step, 1).wait_recv()
            left_wall(0)

        send_y(step, 0, x).wait_recv()
        send_y(step, 1, x).wait_recv()
        here = coefs[step, x + 1]
        rise_x = coefs[step, x + 2] - here
        after = unpacked(edge_in[step, 0, x], 128 - GZ)
        before = unpacked(edge_in[step, 1, x], 0)
        turned_y = pltpu.roll(here, LAYER - GZ, 1)
        next_y = jnp.concatenate(
            [turned_y[:, 0:128], jnp.where(short >= 128 - GZ, after, turned_y[:, 128:256])], 1
        )
        rise_y = valid_y * (next_y - here)
        rise_z = valid_z * (pltpu.roll(here, LAYER - 1, 1) - here)
        rise_edge = has_left * (here[:, 0:128] - before)
        if step == 1:
            rise_x = rise_x + w_x[0, x + 1]
            rise_y = rise_y + w_y[x]
            rise_z = rise_z + w_z[x]
            rise_edge = rise_edge + w_edge[x]
        new_x, new_y, new_z, new_edge = (dual_of(rise) for rise in (rise_x, rise_y, rise_z, rise_edge))
        summed = w_x[step, x] - new_x
        turned_y = pltpu.roll(new_y, GZ, 1)
        prev_y = jnp.concatenate(
            [jnp.where(short < GZ, new_edge, turned_y[:, 0:128]), turned_y[:, 128:256]], 1
        )
        summed = summed + (prev_y - new_y)
        summed = summed + (pltpu.roll(new_z, 1, 1) - new_z)
        w_x[step, x + 1] = new_x
        if step == 0:
            w_y[x] = new_y
            w_z[x] = new_z
            w_edge[x] = new_edge
        return summed

    def total_of(number):
        send_sum(number).wait_recv()
        return sums[number] + partner[number]

    def second(turn, carry):
        x = layer_at(turn)
        coef = eta * total_of(turn)
        pass_on(0, turn, x, coef)
        residual(0, turn, x, coef)
        return carry

    def third(turn, carry):
        x = layer_at(turn)
        summed = smooth(0, turn, x)
        change = total_of(PX + turn) - summed
        first_v[x] = change
        coef = coefs[0, x + 1] + eta * (2.0 * change)
        pass_on(1, turn, x, coef)
        residual(1, turn, x, coef)
        return carry

    def last(turn, carry):
        x = layer_at(turn)
        summed = smooth(1, turn, x)
        change = total_of(2 * PX + turn) - summed
        coef = coefs[1, x + 1] + eta * (2.0 * change - first_v[x])
        coef_out[x] = coef

        @pl.when(turn < PX - 1)
        def _():
            right = stacked(coef)
            mask = mask_of(x)
            for block in range(image.shape[1] // ROWS):
                rows = slice(block * ROWS, (block + 1) * ROWS)
                target = base_out[x, rows, :] - product(split_out[rows, :], right)
                base_out[x, rows, :] = mask * (target - jnp.clip(target, floor, ceiling))

        return carry

    @pl.when(part == 0)
    def _():
        pl.semaphore_wait(barrier, 4)
        signal(all_in, mate)

    @pl.when(part == 1)
    def _():
        pl.semaphore_wait(all_in, 1)

    lax.fori_loop(0, PX, second, 0)
    lax.fori_loop(0, PX, third, 0)
    lax.fori_loop(0, PX, last, 0)

    for number in range(3 * PX - WINDOW, 3 * PX):
        send_sum(number).wait_send()
    for step in range(2):
        for way in range(2):
            send_x(step, way).wait_send()
            for x in range(PX):
                send_y(step, way, x).wait_send()


def finish(base, coef_ref, split_ref, mask_ref, level_ref, coef_out, residual_out, result, out_sem, coef_sem):
    subjects = result.shape[0]
    final = PX - 2

    def columns(x):
        return pl.ds(x * LAYER, LAYER)

    copies = [
        pltpu.make_async_copy(base.at[x], residual_out.at[:, columns(x)], out_sem.at[x])
        for x in range(PX) if x != final
    ]
    copies += [
        pltpu.make_async_copy(coef_ref.at[x], coef_out.at[:, columns(x)], coef_sem.at[x])
        for x in range(PX)
    ]
    for copy in copies:
        copy.start()

    floor, ceiling = level_ref[0:1, 0:1], level_ref[1:2, 0:1]
    right = stacked(coef_ref[final])
    mask = mask_ref[:, columns(final)]
    for block in range(subjects // ROWS):
        rows = slice(block * ROWS, (block + 1) * ROWS)
        target = base[final, rows, :] - product(split_ref[rows, :], right)
        result[rows, :] = mask * (target - jnp.clip(target, floor, ceiling))
    copy = pltpu.make_async_copy(result, residual_out.at[:, columns(final)], out_sem.at[final])
    copy.start()
    for copy in (*copies, copy):
        copy.wait()


def per_device(observed, covariates, voxel_mask, tau_index):
    subjects, voxels = observed.shape
    inputs = [
        pltpu.with_memory_space_constraint(value, pltpu.HBM)
        for value in (observed, covariates.T, voxel_mask.reshape(1, voxels))
    ]
    vmem = pl.BlockSpec(memory_space=pltpu.VMEM)
    smem = pl.BlockSpec(memory_space=pltpu.SMEM)
    hbm = pl.BlockSpec(memory_space=pltpu.HBM)
    dma = pltpu.SemaphoreType.DMA
    made = pl.pallas_call(
        iterate,
        out_shape=(
            pltpu.VMEM((PX, subjects, LAYER), F32),
            pltpu.VMEM((PX, COVARS, LAYER), F32),
            pltpu.VMEM((subjects, 4 * COVARS), BF16),
            pltpu.VMEM((1, voxels), F32),
            pltpu.VMEM((2, 128), F32),
        ),
        in_specs=[hbm, hbm, hbm, smem],
        out_specs=(vmem,) * 5,
        scratch_shapes=[
            pltpu.VMEM((PX, subjects, LAYER), F32),
            pltpu.VMEM((PX, subjects, LAYER), F32),
            pltpu.VMEM((3 * PX, COVARS, LAYER), F32),
            pltpu.VMEM((3 * PX, COVARS, LAYER), F32),
            pltpu.VMEM((2, PX + 2, COVARS, LAYER), F32),
            pltpu.VMEM((PX, COVARS, LAYER), F32),
            pltpu.VMEM((2, PX + 1, COVARS, LAYER), F32),
            pltpu.VMEM((PX, COVARS, LAYER), F32),
            pltpu.VMEM((PX, COVARS, LAYER), F32),
            pltpu.VMEM((PX, COVARS, 128), F32),
            pltpu.VMEM((2, 2, PX, COVARS // 4, 128), F32),
            pltpu.VMEM((2, 2, PX, COVARS // 4, 128), F32),
            pltpu.VMEM((COVARS, COVARS), F32),
            pltpu.VMEM((COVARS, COVARS), F32),
            pltpu.VMEM((2 * COVARS, subjects), BF16),
            pltpu.VMEM((COVARS, subjects), F32),
            pltpu.VMEM((1, voxels), jnp.int32),
            dma((PX,)), dma, dma, dma((3 * PX,)), dma((3 * PX,)), dma((2, 2)), dma((2, 2)),
            dma((2, 2, PX)), dma((2, 2, PX)), dma, dma,
            pltpu.SemaphoreType.REGULAR, pltpu.SemaphoreType.REGULAR,
        ],
        compiler_params=pltpu.CompilerParams(
            collective_id=0, has_side_effects=True, vmem_limit_bytes=40 << 20
        ),
        name="iterate",
    )(*inputs, tau_index)
    return pl.pallas_call(
        finish,
        out_shape=(
            jax.ShapeDtypeStruct((COVARS, voxels), F32),
            jax.ShapeDtypeStruct((subjects, voxels), F32),
        ),
        in_specs=[vmem] * 5,
        out_specs=(hbm, hbm),
        scratch_shapes=[pltpu.VMEM((subjects, LAYER), F32), dma((PX,)), dma((PX,))],
        compiler_params=pltpu.CompilerParams(vmem_limit_bytes=24 << 20),
        name="finish",
    )(*made)


def solution(mesh):
    return jax.shard_map(
        per_device,
        mesh=mesh,
        in_specs=(P("sub", "vox"), P("sub", None), P("vox"), P()),
        out_specs=(P(None, "vox"), P("sub", "vox")),
        check_vma=False,
    )
```

```python
import functools

import jax
import jax.numpy as jnp
from jax import lax
from jax.experimental import pallas as pl
from jax.experimental.pallas import tpu as pltpu
from jax.sharding import PartitionSpec as P

COVARS = 64
PX = 8
PY = 8
GZ = 32
NPY = 8
QUANT = 20
LAYER = PY * GZ
ROWS = 256

penalty_fit = 1.0
penalty_tv = 1.0
tv_weight = 0.05
huber_width = 0.02
BOUND = tv_weight / penalty_tv
RATIO = BOUND / (huber_width + BOUND)

MESH = pl.DeviceIdType.MESH
F32 = jnp.float32
BF16 = jnp.bfloat16


def halves(value):
    high = value.astype(BF16)
    return high, (value - high.astype(F32)).astype(BF16)


def product(left, right):
    return jnp.dot(left, right, preferred_element_type=F32)


def stacked(coef):
    high, low = halves(coef)
    return jnp.concatenate([high, high, low, low], 0)


def dual_of(target):
    return jnp.clip(target * RATIO, -BOUND, BOUND)


def levels(tau_ref):
    quantile = tau_ref[0].astype(F32) / QUANT
    return (quantile - 1.0) / penalty_fit, quantile / penalty_fit


def iterate(
    image_hbm, covs_hbm, mask_hbm, tau_ref,
    base_out, coef_out, split_out, mask_out, level_out,
    image, dual, sums, partner, coefs, first_v, w_x, w_y, w_z, w_edge,
    edge_out, edge_in, gram_out, gram_in, covs_t, covs_ref, mask_ref,
    load_sem, covs_sem, mask_sem, sum_send, sum_recv, x_send, x_recv, y_send, y_recv, gram_send, gram_recv, mate_in, all_in,
):
    part = lax.axis_index("sub")
    place = lax.axis_index("vox")
    pencils = lax.axis_size("vox")
    mate = (1 - part, place)
    right_x = (part, lax.rem(place + NPY, pencils))
    left_x = (part, lax.rem(place + pencils - NPY, pencils))
    right_y = (part, lax.rem(place + 1, pencils))
    left_y = (part, lax.rem(place + pencils - 1, pencils))
    crosses = lax.rem(place, 2)
    far_y = (lax.rem(part + crosses, 2), right_y[1])
    behind_y = (lax.rem(part + 1 - crosses, 2), left_y[1])
    pencil_y = lax.rem(lax.rem(place + NPY // 2, pencils), NPY)

    barrier = pltpu.get_barrier_semaphore()

    def signal(semaphore, device):
        pl.semaphore_signal(semaphore, inc=1, device_id=device, device_id_type=MESH)

    @pl.when(part == 0)
    def _():
        signal(barrier, mate)

    def layer_at(turn):
        return lax.rem(turn + PX - 1, PX)

    def load(x):
        return pltpu.make_async_copy(
            image_hbm.at[:, pl.ds(pl.multiple_of(x * LAYER, LAYER), LAYER)],
            image.at[x], load_sem.at[lax.rem(x, 2)],
        )

    def to_mate(source, target, receipt):
        return pltpu.make_async_remote_copy(
            src_ref=source, dst_ref=target, send_sem=sum_send, recv_sem=receipt,
            device_id=mate, device_id_type=MESH,
        )

    def send_sum(number):
        slot = lax.rem(number, 2 * PX)
        return to_mate(sums.at[number], partner.at[number], sum_recv.at[slot])

    def send_x(step, way):
        source, target, device = ((1, PX + 1, left_x), (PX, 0, right_x))[way]
        return pltpu.make_async_remote_copy(
            src_ref=coefs.at[step, source], dst_ref=coefs.at[step, target],
            send_sem=x_send, recv_sem=x_recv.at[step, way],
            device_id=device, device_id_type=MESH,
        )

    def send_y(step, way, turn):
        return pltpu.make_async_remote_copy(
            src_ref=edge_out.at[step, turn, way], dst_ref=edge_in.at[step, turn, way],
            send_sem=y_send, recv_sem=y_recv.at[step, lax.div(turn, 2)],
            device_id=(left_y, far_y)[way], device_id_type=MESH,
        )

    def both_y(step, turn):
        turns = pl.ds(turn, 2)
        return pltpu.make_async_remote_copy(
            src_ref=edge_out.at[step, turns], dst_ref=edge_in.at[step, turns],
            send_sem=y_send, recv_sem=y_recv.at[step, lax.div(turn, 2)],
            device_id=left_y, device_id_type=MESH,
        )

    send_gram = pltpu.make_async_remote_copy(
        src_ref=gram_out, dst_ref=gram_in, send_sem=gram_send, recv_sem=gram_recv,
        device_id=mate, device_id_type=MESH,
    )

    load_covs = pltpu.make_async_copy(covs_hbm, covs_ref, covs_sem)
    load_mask = pltpu.make_async_copy(mask_hbm, mask_ref, mask_sem)
    load_covs.start()
    load_mask.start()
    for turn in range(2):
        load(layer_at(turn)).start()

    @pl.when(part == 1)
    def _():
        pl.semaphore_wait(barrier, 1)
        signal(mate_in, mate)

    load_covs.wait()
    covs = covs_ref[...]
    high, low = halves(covs)
    covs_t[...] = jnp.concatenate([high, low], 0)
    load_mask.wait()
    mask_out[...] = mask_ref[...].astype(F32)

    lane = lax.broadcasted_iota(jnp.int32, (COVARS, LAYER), 1)
    short = lax.broadcasted_iota(jnp.int32, (COVARS, 128), 1)
    valid_y = ((lane < LAYER - GZ) | (pencil_y < NPY - 1)).astype(F32)
    valid_z = (lax.rem(lane, GZ) < GZ - 1).astype(F32)
    has_left = ((short < GZ) & (pencil_y > 0)).astype(F32)

    def mask_of(x):
        return mask_out[:, pl.ds(pl.multiple_of(x * LAYER, LAYER), LAYER)]

    def packed(block):
        rows = COVARS // 4
        result = block[0:rows]
        for group in range(1, 4):
            moved = pltpu.roll(block[group * rows : (group + 1) * rows], group * GZ, 1)
            result = jnp.where(lax.div(short[0:rows], GZ) == group, moved, result)
        return result

    def unpacked(block, lane_at):
        moved = [(lane_at - group * GZ) % 128 for group in range(4)]
        return jnp.concatenate([pltpu.roll(block, by, 1) if by else block for by in moved], 0)

    def add_up(total, rows, high, low):
        both = product(covs_t[:, rows], high)
        one = product(covs_t[0:COVARS, rows], low)
        term = both[0:COVARS] + both[COVARS:] + one
        return term if total is None else total + term

    def first(turn, carry):
        x = layer_at(turn)
        load(x).wait()

        @pl.when(turn + 2 < PX)
        def _():
            load(layer_at(turn + 2)).start()

        total = None
        for block in range(image.shape[1] // ROWS):
            rows = slice(block * ROWS, (block + 1) * ROWS)
            total = add_up(total, rows, *halves(image[x, rows, :]))
        sums[turn] = total * mask_of(x)

        @pl.when((turn == 0) & (part == 0))
        def _():
            pl.semaphore_wait(mate_in, 1)
            for device in (right_x, left_x, right_y, left_y):
                signal(barrier, device)

        send_sum(turn).start()

        @pl.when(turn == 0)
        def _():
            gram_out[...] = lax.dot_general(
                covs, covs, (((1,), (1,)), ((), ())),
                precision=lax.Precision.HIGHEST, preferred_element_type=F32,
            )
            send_gram.start()

        return carry

    lax.fori_loop(0, PX, first, 0)
    pair = jnp.concatenate([high.astype(F32), low.astype(F32)], 0).T.astype(BF16)
    split_out[...] = jnp.concatenate([pair, pair], 1)
    floor, ceiling = levels(tau_ref)
    level_out[0:1, :] = jnp.full((1, 128), floor, F32)
    level_out[1:2, :] = jnp.full((1, 128), ceiling, F32)

    send_gram.wait()
    gram = gram_out[...] + gram_in[...]
    row_bound = jnp.max(jnp.sum(jnp.abs(gram), axis=1, keepdims=True), axis=0, keepdims=True)
    eta = 1.0 / (penalty_fit * row_bound + 12.0 * penalty_tv)

    def pass_on(step, turn, x, coef):
        coefs[step, x + 1] = coef
        for way, block in ((0, coef[:, 0:128]), (1, pltpu.roll(coef[:, 128:256], GZ, 1))):
            edge_out[step, turn, way] = packed(block)
            send_y(step, way, turn).start()

        @pl.when(turn == 0)
        def _():
            send_x(step, 1).start()

        @pl.when(turn == 1)
        def _():
            send_x(step, 0).start()

    def residual(step, turn, x, coef):
        right = stacked(coef)
        total = None
        for block in range(image.shape[1] // ROWS):
            rows = slice(block * ROWS, (block + 1) * ROWS)
            seen = image[x, rows, :]
            target = seen - product(split_out[rows, :], right)
            if step == 1:
                target = target + dual[x, rows, :]
            new = jnp.clip(target, floor, ceiling)
            if step == 0:
                dual[x, rows, :] = new
            else:
                base_out[x, rows, :] = seen + new
            total = add_up(total, rows, *halves(new))
        number = (step + 1) * PX + turn
        sums[number] = total * mask_of(x)
        send_sum(number).start()

    def smooth(step, turn, x):
        def left_wall(at):
            rise = coefs[step, at + 1] - coefs[step, at]
            if step == 1:
                rise = rise + w_x[0, at]
            w_x[step, at] = dual_of(rise)

        @pl.when(turn == 0)
        def _():
            send_x(step, 0).wait_recv()
            left_wall(PX - 1)

        @pl.when(turn == 1)
        def _():
            send_x(step, 1).wait_recv()
            left_wall(0)

        @pl.when(lax.rem(turn, 2) == 0)
        def _():
            both_y(step, turn).wait_recv()

        here = coefs[step, x + 1]
        rise_x = coefs[step, x + 2] - here
        after = unpacked(edge_in[step, turn, 0], 128 - GZ)
        before = unpacked(edge_in[step, turn, 1], 0)
        turned_y = pltpu.roll(here, LAYER - GZ, 1)
        next_y = jnp.concatenate(
            [turned_y[:, 0:128], jnp.where(short >= 128 - GZ, after, turned_y[:, 128:256])], 1
        )
        rise_y = valid_y * (next_y - here)
        rise_z = valid_z * (pltpu.roll(here, LAYER - 1, 1) - here)
        rise_edge = has_left * (here[:, 0:128] - before)
        if step == 1:
            rise_x = rise_x + w_x[0, x + 1]
            rise_y = rise_y + w_y[x]
            rise_z = rise_z + w_z[x]
            rise_edge = rise_edge + w_edge[x]
        new_x, new_y, new_z, new_edge = (dual_of(rise) for rise in (rise_x, rise_y, rise_z, rise_edge))
        summed = w_x[step, x] - new_x
        turned_y = pltpu.roll(new_y, GZ, 1)
        prev_y = jnp.concatenate(
            [jnp.where(short < GZ, new_edge, turned_y[:, 0:128]), turned_y[:, 128:256]], 1
        )
        summed = summed + (prev_y - new_y)
        summed = summed + (pltpu.roll(new_z, 1, 1) - new_z)
        w_x[step, x + 1] = new_x
        if step == 0:
            w_y[x] = new_y
            w_z[x] = new_z
            w_edge[x] = new_edge
        return summed

    def total_of(number):
        send_sum(number).wait_recv()
        return sums[number] + partner[number]

    def second(turn, carry):
        x = layer_at(turn)
        coef = eta * total_of(turn)
        pass_on(0, turn, x, coef)
        residual(0, turn, x, coef)
        return carry

    def third(turn, carry):
        x = layer_at(turn)
        summed = smooth(0, turn, x)
        change = total_of(PX + turn) - summed
        first_v[x] = change
        coef = coefs[0, x + 1] + eta * (2.0 * change)
        pass_on(1, turn, x, coef)
        residual(1, turn, x, coef)
        return carry

    def last(turn, carry):
        x = layer_at(turn)
        summed = smooth(1, turn, x)
        change = total_of(2 * PX + turn) - summed
        coef = coefs[1, x + 1] + eta * (2.0 * change - first_v[x])
        coef_out[x] = coef

        @pl.when(turn < PX - 1)
        def _():
            right = stacked(coef)
            mask = mask_of(x)
            for block in range(image.shape[1] // ROWS):
                rows = slice(block * ROWS, (block + 1) * ROWS)
                target = base_out[x, rows, :] - product(split_out[rows, :], right)
                base_out[x, rows, :] = mask * (target - jnp.clip(target, floor, ceiling))

        return carry

    @pl.when(part == 0)
    def _():
        pl.semaphore_wait(barrier, 4)
        signal(all_in, mate)

    @pl.when(part == 1)
    def _():
        pl.semaphore_wait(all_in, 1)

    lax.fori_loop(0, PX, second, 0)
    lax.fori_loop(0, PX, third, 0)
    lax.fori_loop(0, PX, last, 0)

    to_mate(sums, partner, sum_recv.at[0]).wait_send()
    pltpu.make_async_remote_copy(
        src_ref=coefs.at[:, pl.ds(1, 2)], dst_ref=coefs.at[:, pl.ds(1, 2)], send_sem=x_send, recv_sem=x_recv.at[0, 0],
        device_id=left_x, device_id_type=MESH,
    ).wait_send()
    pltpu.make_async_remote_copy(
        src_ref=edge_out, dst_ref=edge_in, send_sem=y_send, recv_sem=y_recv.at[0, 0],
        device_id=left_y, device_id_type=MESH,
    ).wait_send()


def finish(base, coef_ref, split_ref, mask_ref, level_ref, coef_out, residual_out, result, out_sem, coef_sem):
    subjects = result.shape[0]
    final = PX - 2

    def columns(x):
        return pl.ds(x * LAYER, LAYER)

    copies = [
        pltpu.make_async_copy(base.at[x], residual_out.at[:, columns(x)], out_sem)
        for x in range(PX) if x != final
    ]
    copies += [
        pltpu.make_async_copy(coef_ref.at[x], coef_out.at[:, columns(x)], coef_sem)
        for x in range(PX)
    ]
    for copy in copies:
        copy.start()

    floor, ceiling = level_ref[0:1, 0:1], level_ref[1:2, 0:1]
    right = stacked(coef_ref[final])
    mask = mask_ref[:, columns(final)]
    for block in range(subjects // ROWS):
        rows = slice(block * ROWS, (block + 1) * ROWS)
        target = base[final, rows, :] - product(split_ref[rows, :], right)
        result[rows, :] = mask * (target - jnp.clip(target, floor, ceiling))
    pltpu.make_async_copy(result, residual_out.at[:, columns(final)], out_sem).start()
    pltpu.make_async_copy(coef_ref, coef_ref, coef_sem).wait()
    pltpu.make_async_copy(base, base, out_sem).wait()


def per_device(observed, covariates, voxel_mask, tau_index):
    subjects, voxels = observed.shape
    inputs = [
        pltpu.with_memory_space_constraint(value, pltpu.HBM)
        for value in (observed, covariates.T, voxel_mask.reshape(1, voxels))
    ]
    vmem = pl.BlockSpec(memory_space=pltpu.VMEM)
    smem = pl.BlockSpec(memory_space=pltpu.SMEM)
    hbm = pl.BlockSpec(memory_space=pltpu.HBM)
    dma = pltpu.SemaphoreType.DMA
    made = pl.pallas_call(
        iterate,
        out_shape=(
            pltpu.VMEM((PX, subjects, LAYER), F32),
            pltpu.VMEM((PX, COVARS, LAYER), F32),
            pltpu.VMEM((subjects, 4 * COVARS), BF16),
            pltpu.VMEM((1, voxels), F32),
            pltpu.VMEM((2, 128), F32),
        ),
        in_specs=[hbm, hbm, hbm, smem],
        out_specs=(vmem,) * 5,
        scratch_shapes=[
            pltpu.VMEM((PX, subjects, LAYER), F32),
            pltpu.VMEM((PX, subjects, LAYER), F32),
            pltpu.VMEM((3 * PX, COVARS, LAYER), F32),
            pltpu.VMEM((3 * PX, COVARS, LAYER), F32),
            pltpu.VMEM((2, PX + 2, COVARS, LAYER), F32),
            pltpu.VMEM((PX, COVARS, LAYER), F32),
            pltpu.VMEM((2, PX + 1, COVARS, LAYER), F32),
            pltpu.VMEM((PX, COVARS, LAYER), F32),
            pltpu.VMEM((PX, COVARS, LAYER), F32),
            pltpu.VMEM((PX, COVARS, 128), F32),
            pltpu.VMEM((2, PX, 2, COVARS // 4, 128), F32),
            pltpu.VMEM((2, PX, 2, COVARS // 4, 128), F32),
            pltpu.VMEM((COVARS, COVARS), F32),
            pltpu.VMEM((COVARS, COVARS), F32),
            pltpu.VMEM((2 * COVARS, subjects), BF16),
            pltpu.VMEM((COVARS, subjects), F32),
            pltpu.VMEM((1, voxels), jnp.int32),
            dma((2,)), dma, dma, dma, dma((2 * PX,)), dma, dma((2, 2)),
            dma, dma((2, PX // 2)), dma, dma,
            pltpu.SemaphoreType.REGULAR, pltpu.SemaphoreType.REGULAR,
        ],
        compiler_params=pltpu.CompilerParams(
            collective_id=0, has_side_effects=True, vmem_limit_bytes=40 << 20
        ),
        name="iterate",
    )(*inputs, tau_index)
    return pl.pallas_call(
        finish,
        out_shape=(
            jax.ShapeDtypeStruct((COVARS, voxels), F32),
            jax.ShapeDtypeStruct((subjects, voxels), F32),
        ),
        in_specs=[vmem] * 5,
        out_specs=(hbm, hbm),
        scratch_shapes=[pltpu.VMEM((subjects, LAYER), F32), dma, dma],
        compiler_params=pltpu.CompilerParams(vmem_limit_bytes=24 << 20),
        name="finish",
    )(*made)


def solution(mesh):
    return jax.shard_map(
        per_device,
        mesh=mesh,
        in_specs=(P("sub", "vox"), P("sub", None), P("vox"), P()),
        out_specs=(P(None, "vox"), P("sub", "vox")),
        check_vma=False,
    )
```
